32 devices in a mesh: seq: 16 (over z, y, x), ch: 2 (over core).
Axes of the slice: x: 2, y: 2, z: 4, core: 2. Of those that a mesh axis runs over, the one named last changes fastest.
Arguments:
- query: bfloat16 [4096, 4096], P('seq', 'ch'), may hold values from -6 to 6
- key_in: bfloat16 [4096, 4096], P('seq', 'ch'), may hold values from -6 to 6
- values: bfloat16 [4096, 4096], P('seq', 'ch'), may hold values from -6 to 6
- cotangent: bfloat16 [4096, 4096], P('seq', 'ch'), may hold values from -6 to 6
- residues: float32 [16, 128], replicated, may hold values from -1.5 to 1.5
- decay_rates: float32 [16, 128], replicated, may hold values from 0.00012207031 to 0.1
Outputs:
- query_grad: bfloat16 [4096, 4096], P('seq', 'ch')
- key_grad: bfloat16 [4096, 4096], P('seq', 'ch')
- value_grad: bfloat16 [4096, 4096], P('seq', 'ch')
- residue_grad: float32 [16, 128], replicated
- rate_grad: float32 [16, 128], replicated
The draws below stay inside these ranges and needn't reach their ends.
All inputs are finite; a program needn't handle non-finite values.
Results may differ from the reference program's by a relative error of at most 0.0012.
Values sent between devices are 32-bit elements; how exact they have to be, the bound alone decides.
A program may use at most 128 MiB of HBM per device.

```python
import math
import jax
import jax.numpy as jnp
from jax import lax

C = 4096
F = 128
M = 16
TOKENS = 4096


def level_of(own_key, shape, pieces, smallest, high):
    def one(dim, parts):
        heights = jax.random.uniform(jax.random.fold_in(jax.random.fold_in(own_key, 6), dim), (parts,), jnp.float32, smallest / len(pieces), high / len(pieces))
        return jnp.repeat(jnp.exp(heights), shape[dim] // parts).reshape((-1,) + (1,) * (len(shape) - dim - 1))

    level = one(*pieces[0])
    for cut in pieces[1:]:
        level = level * one(*cut)
    return level


def scatter_about(rng, extent, width, bound, pieces=(), kind=jnp.bfloat16):
    values = width * jax.random.normal(rng, extent, jnp.float32)
    if pieces:
        values = values * level_of(rng, extent, pieces, -0.22, 0.18)
    return jnp.clip(values, -bound, bound).astype(kind)


def setup_inputs(seed: int = 0) -> dict:
    seeds = jax.random.split(jax.random.key(seed), 7)
    return {
        "query": scatter_about(seeds[0], (TOKENS, C), 1.0, 6.0, ((0, 16), (1, 2))),
        "key_in": scatter_about(seeds[1], (TOKENS, C), 1.0, 6.0, ((0, 16), (1, 2))),
        "values": scatter_about(seeds[2], (TOKENS, C), 1.0, 6.0, ((0, 16), (1, 2))),
        "cotangent": scatter_about(seeds[3], (TOKENS, C), 1.0, 6.0, ((0, 16), (1, 2))),
        "residues": scatter_about(seeds[4], (M, F), M ** -0.5, 1.5, (), jnp.float32),
        "decay_rates": jnp.clip(jnp.exp(jax.random.uniform(seeds[5], (M, F), jnp.float32, math.log(0.00012207031), math.log(0.1))), 0.00012207031, 0.1),
    }


def mode_scale(decay_rates):
    return jnp.sqrt(-jnp.expm1(-2.0 * decay_rates))

def filter_time(residues, decay_rates, positions):
    scale = mode_scale(decay_rates)
    impulse = jnp.zeros((positions.shape[0], residues.shape[1]), jnp.float32)
    for mode_index in range(residues.shape[0]):
        impulse = impulse + (residues[mode_index] * scale[mode_index])[None, :] * jnp.exp(-decay_rates[mode_index][None, :] * positions[:, None])
    return impulse

def filter_sums(filter_grad, residues, decay_rates, positions):
    scale = mode_scale(decay_rates)
    slope = jnp.exp(-2.0 * decay_rates) / scale
    firsts = []
    seconds = []
    for mode_index in range(residues.shape[0]):
        weighted = filter_grad * jnp.exp(-decay_rates[mode_index][None, :] * positions[:, None])
        firsts.append(scale[mode_index] * lax.optimization_barrier(jnp.sum(weighted, axis=0)))
        factor = slope[mode_index][None, :] - scale[mode_index][None, :] * positions[:, None]
        seconds.append(decay_rates[mode_index] * residues[mode_index] * lax.optimization_barrier(jnp.sum(weighted * factor, axis=0)))
    return (jnp.stack(firsts), jnp.stack(seconds))

def reference(query, key_in, values, cotangent, residues, decay_rates):
    length = TOKENS
    padded = 2 * length
    filters = F
    groups = C // F
    positions = jnp.arange(length).astype(jnp.float32)
    impulse = filter_time(residues, decay_rates, positions)
    spec_filter = jnp.fft.rfft(impulse, n=padded, axis=0)

    def one_group(carry, group_index):
        start = (group_index * filters).astype(jnp.int32)
        q_cols = lax.dynamic_slice_in_dim(query, start, filters, 1).astype(jnp.float32)
        k_cols = lax.dynamic_slice_in_dim(key_in, start, filters, 1).astype(jnp.float32)
        v_cols = lax.dynamic_slice_in_dim(values, start, filters, 1).astype(jnp.float32)
        g_cols = lax.dynamic_slice_in_dim(cotangent, start, filters, 1).astype(jnp.float32)
        gated = k_cols * v_cols
        signal_grad = g_cols * q_cols
        spec_gated = jnp.fft.rfft(gated, n=padded, axis=0)
        spec_signal = jnp.fft.rfft(signal_grad, n=padded, axis=0)
        conv = jnp.fft.irfft(spec_gated * spec_filter, n=padded, axis=0)[:length]
        gated_grad = jnp.fft.irfft(spec_signal * jnp.conj(spec_filter), n=padded, axis=0)[:length]
        correlation = jnp.fft.irfft(spec_signal * jnp.conj(spec_gated), n=padded, axis=0)[:length]
        query_grad = (g_cols * conv).astype(jnp.bfloat16)
        key_grad = (gated_grad * v_cols).astype(jnp.bfloat16)
        value_grad = (gated_grad * k_cols).astype(jnp.bfloat16)
        return (carry + correlation, (query_grad, key_grad, value_grad))
    start_grad = jnp.zeros((length, filters), jnp.float32)
    filter_grad, outputs = lax.scan(one_group, start_grad, jnp.arange(groups, dtype=jnp.int32))

    def unstack(stacked):
        return jnp.transpose(stacked, (1, 0, 2)).reshape(length, groups * filters)
    firsts, seconds = filter_sums(filter_grad, residues, decay_rates, positions)
    norm_factor = 1.0 / math.sqrt(length)
    return (unstack(outputs[0]), unstack(outputs[1]), unstack(outputs[2]), firsts * norm_factor, seconds * norm_factor)
```

```python
import functools
import math

import jax
import jax.numpy as jnp
from jax import lax
from jax.experimental import pallas as pl
from jax.experimental.pallas import tpu as pltpu
from jax.sharding import PartitionSpec as P

SUBS = 8
LANES = 128
TILE = 4


def wide(row):
    return jnp.broadcast_to(row, (SUBS, LANES))


def fill_impulse(imp_ref, wgt_ref, dec_ref, length):
    modes = dec_ref.shape[0]
    lag = lax.broadcasted_iota(jnp.int32, (SUBS, LANES), 0)
    for block in range(length // SUBS):
        lags = (lag + block * SUBS).astype(jnp.float32)
        total = jnp.zeros((SUBS, LANES), jnp.float32)
        for m in range(modes):
            rate = dec_ref[m : m + 1, :]
            weight = wgt_ref[m : m + 1, :]
            total = total + weight * jnp.exp(-rate * lags)
        for i in range(SUBS):
            imp_ref[block * SUBS + i] = wide(total[i : i + 1, :])


def split_tokens(nat_ref, out_ref, length):
    for j in range(length):
        out_ref[j] = nat_ref[pl.ds(j, SUBS, stride=length), :]


def join_tokens(nat_ref, pieces, length):
    for j in range(length):
        nat_ref[pl.ds(j, SUBS, stride=length), :] = pieces[j]


def near_lags(u_ref, s_ref, imp_ref, conv, back, corr, length):
    tiles = length // TILE
    for j in range(length):
        conv[j] = jnp.zeros((SUBS, LANES), jnp.float32)
        back[j] = jnp.zeros((SUBS, LANES), jnp.float32)
    for delta in range(tiles):
        lags = [d for d in range(TILE * delta - TILE + 1, TILE * delta + TILE) if d >= 0]
        imp = {d: imp_ref[d] for d in lags}
        sums = {d: corr[d] for d in lags}
        for first in range(tiles - delta):
            sources = range(TILE * first, TILE * first + TILE)
            targets = range(TILE * (first + delta), TILE * (first + delta) + TILE)
            us = {s: u_ref[s] for s in sources}
            ss = {t: s_ref[t] for t in targets}
            cs = {t: conv[t] for t in targets}
            bs = {s: back[s] for s in sources}
            for t in targets:
                for s in sources:
                    if t >= s:
                        cs[t] = cs[t] + imp[t - s] * us[s]
                        bs[s] = bs[s] + imp[t - s] * ss[t]
                        sums[t - s] = sums[t - s] + us[s] * ss[t]
            for t in targets:
                conv[t] = cs[t]
            for s in sources:
                back[s] = bs[s]
        for d in lags:
            corr[d] = sums[d]


def block_states(u_ref, s_ref, dec_ref, modes, length):
    zero = jnp.zeros((SUBS, LANES), jnp.float32)
    decay = [wide(jnp.exp(-dec_ref[m : m + 1, :])) for m in modes]
    hs = [zero for _ in modes]
    h1s = [zero for _ in modes]
    gs = [zero for _ in modes]
    g1s = [zero for _ in modes]
    for j in range(length):
        u = u_ref[j]
        s = s_ref[length - 1 - j]
        for n in range(len(decay)):
            moved = decay[n] * hs[n]
            h1s[n] = decay[n] * h1s[n] + moved
            hs[n] = moved + u
            moved = decay[n] * gs[n]
            g1s[n] = decay[n] * g1s[n] + moved
            gs[n] = moved + s
    out = []
    for n in range(len(decay)):
        moved = decay[n] * hs[n]
        out.append((moved, decay[n] * h1s[n] + moved, gs[n], g1s[n]))
    return out


def local_kernel(
    length, k_ref, v_ref, g_ref, q_ref, wgt_ref, dec_ref,
    conv_ref, back_ref, hin_ref, gin_ref, state_ref, slope_ref, sums_ref,
    nat_ref, u_ref, s_ref, imp_ref, corr_ref, first_ref, second_ref,
):
    group = pl.program_id(0)
    modes = dec_ref.shape[0]

    @pl.when(group == 0)
    def _():
        fill_impulse(imp_ref, wgt_ref, dec_ref, length)
        corr_ref[...] = jnp.zeros_like(corr_ref)
        first_ref[...] = jnp.zeros_like(first_ref)
        second_ref[...] = jnp.zeros_like(second_ref)

    nat_ref[...] = k_ref[...].astype(jnp.float32) * v_ref[...].astype(jnp.float32)
    split_tokens(nat_ref, u_ref, length)
    nat_ref[...] = g_ref[...].astype(jnp.float32) * q_ref[...].astype(jnp.float32)
    split_tokens(nat_ref, s_ref, length)

    sub = lax.broadcasted_iota(jnp.int32, (SUBS, LANES), 0)
    half = modes // 2
    for start in range(0, modes, half):
        ids = range(start, start + half)
        for m, (h, h1, g, g1) in zip(ids, block_states(u_ref, s_ref, dec_ref, ids, length)):
            rate = wide(dec_ref[m : m + 1, :])
            ih, ih1, ig, ig1 = h, h1, g, g1
            step = 1
            while step < SUBS:
                span = float(step * length)
                power = jnp.exp(-span * rate)
                up = jnp.where(sub >= step, power, 0.0)
                down = jnp.where(sub < SUBS - step, power, 0.0)
                rh = pltpu.roll(ih, step, 0)
                rh1 = pltpu.roll(ih1, step, 0)
                ih1 = ih1 + up * (rh1 + span * rh)
                ih = ih + up * rh
                rg = pltpu.roll(ig, SUBS - step, 0)
                rg1 = pltpu.roll(ig1, SUBS - step, 0)
                ig1 = ig1 + down * (rg1 + span * rg)
                ig = ig + down * rg
                step *= 2
            hin = jnp.where(sub >= 1, pltpu.roll(ih, 1, 0), 0.0)
            h1in = jnp.where(sub >= 1, pltpu.roll(ih1, 1, 0), 0.0)
            gin = jnp.where(sub < SUBS - 1, pltpu.roll(ig, SUBS - 1, 0), 0.0)
            hin_ref[0, m] = hin
            gin_ref[0, m] = gin
            state_ref[0, 0, m : m + 1, :] = ih[SUBS - 1 :, :]
            state_ref[0, 1, m : m + 1, :] = ig[:1, :]
            slope_ref[0, 0, m : m + 1, :] = ih1[SUBS - 1 :, :]
            slope_ref[0, 1, m : m + 1, :] = ig1[:1, :]
            first_ref[m] += g * hin
            second_ref[m] += g1 * hin + g * h1in

    near_lags(u_ref, s_ref, imp_ref, conv_ref.at[0], back_ref.at[0], corr_ref, length)

    @pl.when(group == pl.num_programs(0) - 1)
    def _():
        corr = [jnp.sum(corr_ref[j], axis=0, keepdims=True) for j in range(length)]
        packs = [jnp.concatenate(corr[b : b + SUBS], axis=0) for b in range(0, length, SUBS)]
        for m in range(modes):
            rate = dec_ref[m : m + 1, :]
            first = first_ref[m]
            second = second_ref[m]
            for b in range(len(packs)):
                lags = (sub + b * SUBS).astype(jnp.float32)
                term = packs[b] * jnp.exp(-rate * lags)
                first = first + term
                second = second + term * lags
            sums_ref[0, m : m + 1, :] = jnp.sum(first, axis=0, keepdims=True)
            sums_ref[1, m : m + 1, :] = jnp.sum(second, axis=0, keepdims=True)


def local_pass(query, key_in, values, cotangent, weights, decay_rates):
    rows, channels = query.shape
    modes, filters = decay_rates.shape
    groups = channels // filters
    length = rows // SUBS
    column = pl.BlockSpec((rows, filters), lambda g: (0, g))
    small = pl.BlockSpec((modes, filters), lambda g: (0, 0))
    f32 = jnp.float32
    piece = pl.BlockSpec((1, length, SUBS, filters), lambda g: (g, 0, 0, 0))
    inner = pl.BlockSpec((1, modes, SUBS, filters), lambda g: (g, 0, 0, 0))
    pair = pl.BlockSpec((1, 2, modes, filters), lambda g: (g, 0, 0, 0))
    return pl.pallas_call(
        functools.partial(local_kernel, length),
        grid=(groups,),
        in_specs=[column] * 4 + [small] * 2,
        out_specs=[piece, piece, inner, inner, pair, pair,
                   pl.BlockSpec((2, modes, filters), lambda g: (0, 0, 0))],
        out_shape=[
            jax.ShapeDtypeStruct((groups, length, SUBS, filters), f32),
            jax.ShapeDtypeStruct((groups, length, SUBS, filters), f32),
            jax.ShapeDtypeStruct((groups, modes, SUBS, filters), f32),
            jax.ShapeDtypeStruct((groups, modes, SUBS, filters), f32),
            jax.ShapeDtypeStruct((groups, 2, modes, filters), f32),
            jax.ShapeDtypeStruct((groups, 2, modes, filters), f32),
            jax.ShapeDtypeStruct((2, modes, filters), f32),
        ],
        scratch_shapes=[
            pltpu.VMEM((rows, filters), f32),
            pltpu.VMEM((length, SUBS, filters), f32),
            pltpu.VMEM((length, SUBS, filters), f32),
            pltpu.VMEM((length, SUBS, filters), f32),
            pltpu.VMEM((length, SUBS, filters), f32),
            pltpu.VMEM((modes, SUBS, filters), f32),
            pltpu.VMEM((modes, SUBS, filters), f32),
        ],
        compiler_params=pltpu.CompilerParams(vmem_limit_bytes=32 * 1024 * 1024),
        name="local_pass",
    )(key_in, values, cotangent, query, weights, decay_rates)


def owner_kernel(span, x_ref, dec_ref, y_ref, first_ref, second_ref):
    devices = x_ref.shape[0]
    power = jnp.exp(-span * dec_ref[...])
    state = jnp.zeros_like(dec_ref[...])
    slope = state
    first = state
    second = state
    for d in range(devices):
        y_ref[d, 0] = state
        first = first + x_ref[d, 1] * state
        second = second + x_ref[d, 1] * slope
        slope = power * (slope + span * state)
        state = power * state + x_ref[d, 0]
    state = jnp.zeros_like(dec_ref[...])
    for d in reversed(range(devices)):
        y_ref[d, 1] = state
        state = power * state + x_ref[d, 1]
    first_ref[...] = first
    second_ref[...] = second


def owner_pass(received, rates, span):
    f32 = jnp.float32
    return pl.pallas_call(
        functools.partial(owner_kernel, span),
        out_shape=[
            jax.ShapeDtypeStruct(received.shape, f32),
            jax.ShapeDtypeStruct(rates.shape, f32),
            jax.ShapeDtypeStruct(rates.shape, f32),
        ],
        name="owner_pass",
    )(received, rates)


def finish_kernel(
    length, k_ref, v_ref, g_ref, wgt_ref, dec_ref, conv_ref, back_ref, hin_ref, gin_ref, far_ref,
    dq_ref, dk_ref, dv_ref, nat_ref,
):
    modes = dec_ref.shape[0]
    sub = lax.broadcasted_iota(jnp.int32, (SUBS, LANES), 0).astype(jnp.float32)
    decay = []
    ahead = []
    behind = []
    for m in range(modes):
        rate = dec_ref[m : m + 1, :]
        weight = wgt_ref[m : m + 1, :]
        decay.append(wide(jnp.exp(-rate)))
        before = jnp.exp(-rate * (sub * float(length)))
        after = jnp.exp(-rate * ((SUBS - 1.0 - sub) * float(length)))
        ahead.append(weight * (hin_ref[0, m] + before * far_ref[0, 0, m : m + 1, :]))
        behind.append(weight * (gin_ref[0, m] + after * far_ref[0, 1, m : m + 1, :]))

    def total(parts):
        while len(parts) > 1:
            parts = [sum(parts[i : i + 2]) for i in range(0, len(parts), 2)]
        return parts[0]

    for j in range(length):
        nat_ref[pl.ds(j, SUBS, stride=length), :] = conv_ref[0, j] + total(ahead)
        ahead = [x * a for x, a in zip(ahead, decay)]
    dq_ref[...] = (g_ref[...].astype(jnp.float32) * nat_ref[...]).astype(jnp.bfloat16)
    for j in reversed(range(length)):
        behind = [x * a for x, a in zip(behind, decay)]
        nat_ref[pl.ds(j, SUBS, stride=length), :] = back_ref[0, j] + total(behind)
    dk_ref[...] = (v_ref[...].astype(jnp.float32) * nat_ref[...]).astype(jnp.bfloat16)
    dv_ref[...] = (k_ref[...].astype(jnp.float32) * nat_ref[...]).astype(jnp.bfloat16)


def finish_pass(key_in, values, cotangent, weights, decay_rates, conv, back, hin, gin, far):
    rows, channels = key_in.shape
    modes, filters = decay_rates.shape
    groups = channels // filters
    length = rows // SUBS
    column = pl.BlockSpec((rows, filters), lambda g: (0, g))
    small = pl.BlockSpec((modes, filters), lambda g: (0, 0))
    piece = pl.BlockSpec((1, length, SUBS, filters), lambda g: (g, 0, 0, 0))
    inner = pl.BlockSpec((1, modes, SUBS, filters), lambda g: (g, 0, 0, 0))
    pair = pl.BlockSpec((1, 2, modes, filters), lambda g: (g, 0, 0, 0))
    return pl.pallas_call(
        functools.partial(finish_kernel, length),
        grid=(groups,),
        in_specs=[column] * 3 + [small] * 2 + [piece, piece, inner, inner, pair],
        out_specs=[column] * 3,
        out_shape=[jax.ShapeDtypeStruct((rows, channels), jnp.bfloat16)] * 3,
        scratch_shapes=[pltpu.VMEM((rows, filters), jnp.float32)],
        compiler_params=pltpu.CompilerParams(vmem_limit_bytes=32 * 1024 * 1024),
        name="finish_pass",
    )(key_in, values, cotangent, weights, decay_rates, conv, back, hin, gin, far)


def shards(query, key_in, values, cotangent, residues, decay_rates):
    devices = lax.axis_size("seq")
    me = lax.axis_index("seq")
    rows, channels = query.shape
    modes, filters = decay_rates.shape
    groups = channels // filters
    share = groups * modes // devices
    scale = jnp.sqrt(-jnp.expm1(-2.0 * decay_rates))
    weights = residues * scale
    conv, back, hin, gin, states, slopes, sums = local_pass(
        query, key_in, values, cotangent, weights, decay_rates
    )
    sent = states.transpose(0, 2, 1, 3).reshape(devices, share, 2, filters).transpose(0, 2, 1, 3)
    received = lax.all_to_all(sent, "seq", split_axis=0, concat_axis=0, tiled=True)
    row_rates = jnp.tile(decay_rates, (groups, 1)).reshape(devices, share, filters)
    own_rates = lax.dynamic_index_in_dim(row_rates, me, 0, keepdims=False)
    answer, first, second = owner_pass(received, own_rates, float(rows))
    far = lax.all_to_all(answer, "seq", split_axis=0, concat_axis=0, tiled=True)
    far = far.transpose(0, 2, 1, 3).reshape(groups, modes, 2, filters).transpose(0, 2, 1, 3)
    crossing = jnp.sum(slopes[:, 1] * far[:, 0] + slopes[:, 0] * far[:, 1], axis=0)
    owned = jnp.zeros((2, groups * modes, filters), jnp.float32)
    owned = lax.dynamic_update_slice(owned, jnp.stack([first, second]), (0, me * share, 0))
    owned = owned.reshape(2, groups, modes, filters).sum(1)
    zeroth = sums[0] + owned[0]
    moment = sums[1] + owned[1] + crossing
    zeroth, moment = lax.psum((zeroth, moment), ("seq", "ch"))
    query_grad, key_grad, value_grad = finish_pass(
        key_in, values, cotangent, weights, decay_rates, conv, back, hin, gin, far
    )
    norm_factor = 1.0 / math.sqrt(devices * rows)
    slope = jnp.exp(-2.0 * decay_rates) / scale
    residue_grad = scale * zeroth * norm_factor
    rate_grad = decay_rates * residues * (slope * zeroth - scale * moment) * norm_factor
    return (query_grad, key_grad, value_grad, residue_grad, rate_grad)


def solution(mesh):
    in_specs = (P("seq", "ch"), P("seq", "ch"), P("seq", "ch"), P("seq", "ch"), P(), P())
    out_specs = (P("seq", "ch"), P("seq", "ch"), P("seq", "ch"), P(), P())
    return jax.shard_map(shards, mesh=mesh, in_specs=in_specs, out_specs=out_specs, check_vma=False)
```

```python
import functools
import math

import jax
import jax.numpy as jnp
from jax import lax
from jax.experimental import pallas as pl
from jax.experimental.pallas import tpu as pltpu
from jax.sharding import PartitionSpec as P

SUBS = 8
LANES = 128
TILE = 4


def wide(row):
    return jnp.broadcast_to(row, (SUBS, LANES))


def fill_impulse(imp_ref, wgt_ref, dec_ref, length):
    modes = dec_ref.shape[0]
    lag = lax.broadcasted_iota(jnp.int32, (SUBS, LANES), 0)
    for block in range(length // SUBS):
        lags = (lag + block * SUBS).astype(jnp.float32)
        total = jnp.zeros((SUBS, LANES), jnp.float32)
        for m in range(modes):
            rate = dec_ref[m : m + 1, :]
            weight = wgt_ref[m : m + 1, :]
            total = total + weight * jnp.exp(-rate * lags)
        for i in range(SUBS):
            imp_ref[block * SUBS + i] = wide(total[i : i + 1, :])


def split_tokens(nat_ref, out_ref, length):
    for j in range(length):
        out_ref[j] = nat_ref[pl.ds(j, SUBS, stride=length), :]


def join_tokens(nat_ref, pieces, length):
    for j in range(length):
        nat_ref[pl.ds(j, SUBS, stride=length), :] = pieces[j]


def near_lags(u_ref, s_ref, imp_ref, conv, back, corr, length):
    tiles = length // TILE
    for j in range(length):
        conv[j] = jnp.zeros((SUBS, LANES), jnp.float32)
        back[j] = jnp.zeros((SUBS, LANES), jnp.float32)
    for delta in range(tiles):
        lags = [d for d in range(TILE * delta - TILE + 1, TILE * delta + TILE) if d >= 0]
        imp = {d: imp_ref[d] for d in lags}
        sums = {d: corr[d] for d in lags}
        for first in range(tiles - delta):
            sources = range(TILE * first, TILE * first + TILE)
            targets = range(TILE * (first + delta), TILE * (first + delta) + TILE)
            us = {s: u_ref[s] for s in sources}
            ss = {t: s_ref[t] for t in targets}
            cs = {t: conv[t] for t in targets}
            bs = {s: back[s] for s in sources}
            for t in targets:
                for s in sources:
                    if t >= s:
                        cs[t] = cs[t] + imp[t - s] * us[s]
                        bs[s] = bs[s] + imp[t - s] * ss[t]
                        sums[t - s] = sums[t - s] + us[s] * ss[t]
            for t in targets:
                conv[t] = cs[t]
            for s in sources:
                back[s] = bs[s]
        for d in lags:
            corr[d] = sums[d]


def block_states(u_ref, s_ref, dec_ref, modes, length):
    zero = jnp.zeros((SUBS, LANES), jnp.float32)
    decay = [wide(jnp.exp(-dec_ref[m : m + 1, :])) for m in modes]
    hs = [zero for _ in modes]
    h1s = [zero for _ in modes]
    gs = [zero for _ in modes]
    g1s = [zero for _ in modes]
    for j in range(length):
        u = u_ref[j]
        s = s_ref[length - 1 - j]
        for n in range(len(decay)):
            moved = decay[n] * hs[n]
            h1s[n] = decay[n] * h1s[n] + moved
            hs[n] = moved + u
            moved = decay[n] * gs[n]
            g1s[n] = decay[n] * g1s[n] + moved
            gs[n] = moved + s
    out = []
    for n in range(len(decay)):
        moved = decay[n] * hs[n]
        out.append((moved, decay[n] * h1s[n] + moved, gs[n], g1s[n]))
    return out


def local_kernel(
    length, k_ref, v_ref, g_ref, q_ref, wgt_ref, dec_ref,
    conv_ref, back_ref, hin_ref, gin_ref, state_ref, slope_ref, sums_ref,
    nat_ref, u_ref, s_ref, imp_ref, corr_ref, first_ref, second_ref,
):
    group = pl.program_id(0)
    modes = dec_ref.shape[0]

    @pl.when(group == 0)
    def _():
        fill_impulse(imp_ref, wgt_ref, dec_ref, length)
        corr_ref[...] = jnp.zeros_like(corr_ref)
        first_ref[...] = jnp.zeros_like(first_ref)
        second_ref[...] = jnp.zeros_like(second_ref)

    nat_ref[...] = k_ref[...].astype(jnp.float32) * v_ref[...].astype(jnp.float32)
    split_tokens(nat_ref, u_ref, length)
    nat_ref[...] = g_ref[...].astype(jnp.float32) * q_ref[...].astype(jnp.float32)
    split_tokens(nat_ref, s_ref, length)

    sub = lax.broadcasted_iota(jnp.int32, (SUBS, LANES), 0)
    half = modes // 2
    for start in range(0, modes, half):
        ids = range(start, start + half)
        for m, (h, h1, g, g1) in zip(ids, block_states(u_ref, s_ref, dec_ref, ids, length)):
            rate = wide(dec_ref[m : m + 1, :])
            ih, ih1, ig, ig1 = h, h1, g, g1
            step = 1
            while step < SUBS:
                span = float(step * length)
                power = jnp.exp(-span * rate)
                up = jnp.where(sub >= step, power, 0.0)
                down = jnp.where(sub < SUBS - step, power, 0.0)
                rh = pltpu.roll(ih, step, 0)
                rh1 = pltpu.roll(ih1, step, 0)
                ih1 = ih1 + up * (rh1 + span * rh)
                ih = ih + up * rh
                rg = pltpu.roll(ig, SUBS - step, 0)
                rg1 = pltpu.roll(ig1, SUBS - step, 0)
                ig1 = ig1 + down * (rg1 + span * rg)
                ig = ig + down * rg
                step *= 2
            hin = jnp.where(sub >= 1, pltpu.roll(ih, 1, 0), 0.0)
            h1in = jnp.where(sub >= 1, pltpu.roll(ih1, 1, 0), 0.0)
            gin = jnp.where(sub < SUBS - 1, pltpu.roll(ig, SUBS - 1, 0), 0.0)
            hin_ref[0, m] = hin
            gin_ref[0, m] = gin
            state_ref[0, 0, m : m + 1, :] = ih[SUBS - 1 :, :]
            state_ref[0, 1, m : m + 1, :] = ig[:1, :]
            slope_ref[0, 0, m : m + 1, :] = ih1[SUBS - 1 :, :]
            slope_ref[0, 1, m : m + 1, :] = ig1[:1, :]
            first_ref[m] += g * hin
            second_ref[m] += g1 * hin + g * h1in

    near_lags(u_ref, s_ref, imp_ref, conv_ref.at[0], back_ref.at[0], corr_ref, length)

    @pl.when(group == pl.num_programs(0) - 1)
    def _():
        corr = [jnp.sum(corr_ref[j], axis=0, keepdims=True) for j in range(length)]
        packs = [jnp.concatenate(corr[b : b + SUBS], axis=0) for b in range(0, length, SUBS)]
        for m in range(modes):
            rate = dec_ref[m : m + 1, :]
            first = first_ref[m]
            second = second_ref[m]
            for b in range(len(packs)):
                lags = (sub + b * SUBS).astype(jnp.float32)
                term = packs[b] * jnp.exp(-rate * lags)
                first = first + term
                second = second + term * lags
            sums_ref[0, m : m + 1, :] = jnp.sum(first, axis=0, keepdims=True)
            sums_ref[1, m : m + 1, :] = jnp.sum(second, axis=0, keepdims=True)


def local_pass(query, key_in, values, cotangent, weights, decay_rates):
    rows, channels = query.shape
    modes, filters = decay_rates.shape
    groups = channels // filters
    length = rows // SUBS
    column = pl.BlockSpec((rows, filters), lambda g: (0, g))
    small = pl.BlockSpec((modes, filters), lambda g: (0, 0))
    f32 = jnp.float32
    piece = pl.BlockSpec((1, length, SUBS, filters), lambda g: (g, 0, 0, 0))
    inner = pl.BlockSpec((1, modes, SUBS, filters), lambda g: (g, 0, 0, 0))
    pair = pl.BlockSpec((1, 2, modes, filters), lambda g: (g, 0, 0, 0))
    return pl.pallas_call(
        functools.partial(local_kernel, length),
        grid=(groups,),
        in_specs=[column] * 4 + [small] * 2,
        out_specs=[piece, piece, inner, inner, pair, pair,
                   pl.BlockSpec((2, modes, filters), lambda g: (0, 0, 0))],
        out_shape=[
            jax.ShapeDtypeStruct((groups, length, SUBS, filters), f32),
            jax.ShapeDtypeStruct((groups, length, SUBS, filters), f32),
            jax.ShapeDtypeStruct((groups, modes, SUBS, filters), f32),
            jax.ShapeDtypeStruct((groups, modes, SUBS, filters), f32),
            jax.ShapeDtypeStruct((groups, 2, modes, filters), f32),
            jax.ShapeDtypeStruct((groups, 2, modes, filters), f32),
            jax.ShapeDtypeStruct((2, modes, filters), f32),
        ],
        scratch_shapes=[
            pltpu.VMEM((rows, filters), f32),
            pltpu.VMEM((length, SUBS, filters), f32),
            pltpu.VMEM((length, SUBS, filters), f32),
            pltpu.VMEM((length, SUBS, filters), f32),
            pltpu.VMEM((length, SUBS, filters), f32),
            pltpu.VMEM((modes, SUBS, filters), f32),
            pltpu.VMEM((modes, SUBS, filters), f32),
        ],
        compiler_params=pltpu.CompilerParams(vmem_limit_bytes=60 * 1024 * 1024),
        name="local_pass",
    )(key_in, values, cotangent, query, weights, decay_rates)


def owner_kernel(span, x_ref, dec_ref, y_ref, first_ref, second_ref):
    devices = x_ref.shape[0]
    power = jnp.exp(-span * dec_ref[...])
    state = jnp.zeros_like(dec_ref[...])
    slope = state
    first = state
    second = state
    for d in range(devices):
        y_ref[d, 0] = state
        first = first + x_ref[d, 1] * state
        second = second + x_ref[d, 1] * slope
        slope = power * (slope + span * state)
        state = power * state + x_ref[d, 0]
    state = jnp.zeros_like(dec_ref[...])
    for d in reversed(range(devices)):
        y_ref[d, 1] = state
        state = power * state + x_ref[d, 1]
    first_ref[...] = first
    second_ref[...] = second


def owner_pass(received, rates, span):
    f32 = jnp.float32
    return pl.pallas_call(
        functools.partial(owner_kernel, span),
        out_shape=[
            jax.ShapeDtypeStruct(received.shape, f32),
            jax.ShapeDtypeStruct(rates.shape, f32),
            jax.ShapeDtypeStruct(rates.shape, f32),
        ],
        name="owner_pass",
    )(received, rates)


def exchange_kernel(
    span, x_ref, slope_ref, sums_ref, dec_ref, far_ref, total_ref,
    got, ans, back, part, red, mine, gath,
    send1, recv1, send2, recv2, send3, recv3, send4, recv4,
):
    devices = x_ref.shape[0]
    cores = gath.shape[0] // devices
    everyone = devices * cores
    me = lax.axis_index("seq")
    ch = lax.axis_index("ch")
    my = ch * devices + me
    mesh_ids = pl.DeviceIdType.MESH

    def seq_copy(source, target, sends, recvs, peer, slot):
        return pltpu.make_async_remote_copy(
            src_ref=source.at[peer], dst_ref=target.at[slot], send_sem=sends.at[peer],
            recv_sem=recvs.at[slot], device_id=(peer, ch), device_id_type=mesh_ids,
        )

    def swap_start(source, target, sends, recvs):
        def body(step, carry):
            peer = lax.rem(me + step, devices)
            seq_copy(source, target, sends, recvs, peer, me).start()
            return carry

        lax.fori_loop(1, devices, body, 0)

    def swap_wait(source, target, sends, recvs):
        def body(step, carry):
            peer = lax.rem(me + step, devices)
            seq_copy(source, target, sends, recvs, peer, peer).wait()
            return carry

        lax.fori_loop(1, devices, body, 0)

    barrier = pltpu.get_barrier_semaphore()

    def greet(step, carry):
        other = lax.rem(my + step, everyone)
        pl.semaphore_signal(
            barrier, inc=1, device_id=(lax.rem(other, devices), other // devices),
            device_id_type=mesh_ids,
        )
        return carry

    lax.fori_loop(1, everyone, greet, 0)
    pl.semaphore_wait(barrier, everyone - 1)

    swap_start(x_ref, got, send1, recv1)
    got[me] = x_ref[me]
    power = jnp.exp(-span * dec_ref[...])
    swap_wait(x_ref, got, send1, recv1)
    zero = jnp.zeros_like(power)
    state, slope, first, second = zero, zero, zero, zero
    for d in range(devices):
        ans[d, 0] = state
        first = first + got[d, 1] * state
        second = second + got[d, 1] * slope
        slope = power * (slope + span * state)
        state = power * state + got[d, 0]
    state = zero
    for d in reversed(range(devices)):
        ans[d, 1] = state
        state = power * state + got[d, 1]

    swap_start(ans, back, send2, recv2)
    back[me] = ans[me]
    swap_wait(ans, back, send2, recv2)
    first = first + sums_ref[0]
    second = second + sums_ref[1]
    for d in range(devices):
        second = second + slope_ref[d, 1] * back[d, 0] + slope_ref[d, 0] * back[d, 1]
        far_ref[d] = back[d]

    rows = part.shape[1]
    half = devices // 2
    for d in range(half):
        part[d] = first[d * rows : (d + 1) * rows, :]
        part[half + d] = second[d * rows : (d + 1) * rows, :]
    swap_start(part, red, send3, recv3)
    red[me] = part[me]
    swap_wait(part, red, send3, recv3)
    total = red[0]
    for d in range(1, devices):
        total = total + red[d]
    mine[...] = total
    gath[my] = total

    def all_copy(other, slot):
        return pltpu.make_async_remote_copy(
            src_ref=mine, dst_ref=gath.at[slot], send_sem=send4.at[other], recv_sem=recv4.at[slot],
            device_id=(lax.rem(other, devices), other // devices), device_id_type=mesh_ids,
        )

    def spread(step, carry):
        all_copy(lax.rem(my + step, everyone), my).start()
        return carry

    def collect(step, carry):
        other = lax.rem(my + step, everyone)
        all_copy(other, other).wait()
        return carry

    lax.fori_loop(1, everyone, spread, 0)
    lax.fori_loop(1, everyone, collect, 0)
    for d in range(devices):
        total = gath[d]
        for c in range(1, cores):
            total = total + gath[c * devices + d]
        total_ref[d] = total


def exchange_pass(states, slopes, sums, decay_rates, span):
    devices = lax.axis_size("seq")
    everyone = devices * lax.axis_size("ch")
    modes, filters = decay_rates.shape
    rows = 2 * modes // devices
    f32 = jnp.float32
    sem = pltpu.SemaphoreType.DMA
    vmem = pl.BlockSpec(memory_space=pltpu.VMEM)
    far, total = pl.pallas_call(
        functools.partial(exchange_kernel, span),
        in_specs=[vmem] * 4,
        out_specs=[vmem] * 2,
        out_shape=[
            jax.ShapeDtypeStruct(states.shape, f32),
            jax.ShapeDtypeStruct((devices, rows, filters), f32),
        ],
        scratch_shapes=[
            pltpu.VMEM(states.shape, f32),
            pltpu.VMEM(states.shape, f32),
            pltpu.VMEM(states.shape, f32),
            pltpu.VMEM((devices, rows, filters), f32),
            pltpu.VMEM((devices, rows, filters), f32),
            pltpu.VMEM((rows, filters), f32),
            pltpu.VMEM((everyone, rows, filters), f32),
        ]
        + [sem((devices,))] * 6
        + [sem((everyone,))] * 2,
        compiler_params=pltpu.CompilerParams(
            collective_id=0, has_side_effects=True, vmem_limit_bytes=60 * 1024 * 1024
        ),
        name="exchange_pass",
    )(states, slopes, sums, decay_rates)
    total = total.reshape(2, modes, filters)
    return far, total[0], total[1]


def plain_exchange(states, slopes, sums, decay_rates, span):
    devices = lax.axis_size("seq")
    me = lax.axis_index("seq")
    groups = states.shape[0]
    modes, filters = decay_rates.shape
    share = groups * modes // devices
    sent = states.transpose(0, 2, 1, 3).reshape(devices, share, 2, filters).transpose(0, 2, 1, 3)
    received = lax.all_to_all(sent, "seq", split_axis=0, concat_axis=0, tiled=True)
    row_rates = jnp.tile(decay_rates, (groups, 1)).reshape(devices, share, filters)
    own_rates = lax.dynamic_index_in_dim(row_rates, me, 0, keepdims=False)
    answer, first, second = owner_pass(received, own_rates, span)
    far = lax.all_to_all(answer, "seq", split_axis=0, concat_axis=0, tiled=True)
    far = far.transpose(0, 2, 1, 3).reshape(groups, modes, 2, filters).transpose(0, 2, 1, 3)
    crossing = jnp.sum(slopes[:, 1] * far[:, 0] + slopes[:, 0] * far[:, 1], axis=0)
    owned = jnp.zeros((2, groups * modes, filters), jnp.float32)
    owned = lax.dynamic_update_slice(owned, jnp.stack([first, second]), (0, me * share, 0))
    owned = owned.reshape(2, groups, modes, filters).sum(1)
    zeroth = sums[0] + owned[0]
    moment = sums[1] + owned[1] + crossing
    zeroth, moment = lax.psum((zeroth, moment), ("seq", "ch"))
    return far, zeroth, moment


def finish_kernel(
    length, k_ref, v_ref, g_ref, wgt_ref, dec_ref, conv_ref, back_ref, hin_ref, gin_ref, far_ref,
    dq_ref, dk_ref, dv_ref, nat_ref,
):
    modes = dec_ref.shape[0]
    sub = lax.broadcasted_iota(jnp.int32, (SUBS, LANES), 0).astype(jnp.float32)
    decay = []
    ahead = []
    behind = []
    for m in range(modes):
        rate = dec_ref[m : m + 1, :]
        weight = wgt_ref[m : m + 1, :]
        decay.append(wide(jnp.exp(-rate)))
        before = jnp.exp(-rate * (sub * float(length)))
        after = jnp.exp(-rate * ((SUBS - 1.0 - sub) * float(length)))
        ahead.append(weight * (hin_ref[0, m] + before * far_ref[0, 0, m : m + 1, :]))
        behind.append(weight * (gin_ref[0, m] + after * far_ref[0, 1, m : m + 1, :]))

    def total(parts):
        while len(parts) > 1:
            parts = [sum(parts[i : i + 2]) for i in range(0, len(parts), 2)]
        return parts[0]

    for j in range(length):
        nat_ref[pl.ds(j, SUBS, stride=length), :] = conv_ref[0, j] + total(ahead)
        ahead = [x * a for x, a in zip(ahead, decay)]
    dq_ref[...] = (g_ref[...].astype(jnp.float32) * nat_ref[...]).astype(jnp.bfloat16)
    for j in reversed(range(length)):
        behind = [x * a for x, a in zip(behind, decay)]
        nat_ref[pl.ds(j, SUBS, stride=length), :] = back_ref[0, j] + total(behind)
    dk_ref[...] = (v_ref[...].astype(jnp.float32) * nat_ref[...]).astype(jnp.bfloat16)
    dv_ref[...] = (k_ref[...].astype(jnp.float32) * nat_ref[...]).astype(jnp.bfloat16)


def finish_pass(key_in, values, cotangent, weights, decay_rates, conv, back, hin, gin, far):
    rows, channels = key_in.shape
    modes, filters = decay_rates.shape
    groups = channels // filters
    length = rows // SUBS
    column = pl.BlockSpec((rows, filters), lambda g: (0, g))
    small = pl.BlockSpec((modes, filters), lambda g: (0, 0))
    piece = pl.BlockSpec((1, length, SUBS, filters), lambda g: (g, 0, 0, 0))
    inner = pl.BlockSpec((1, modes, SUBS, filters), lambda g: (g, 0, 0, 0))
    pair = pl.BlockSpec((1, 2, modes, filters), lambda g: (g, 0, 0, 0))
    return pl.pallas_call(
        functools.partial(finish_kernel, length),
        grid=(groups,),
        in_specs=[column] * 3 + [small] * 2 + [piece, piece, inner, inner, pair],
        out_specs=[column] * 3,
        out_shape=[jax.ShapeDtypeStruct((rows, channels), jnp.bfloat16)] * 3,
        scratch_shapes=[pltpu.VMEM((rows, filters), jnp.float32)],
        compiler_params=pltpu.CompilerParams(vmem_limit_bytes=60 * 1024 * 1024),
        name="finish_pass",
    )(key_in, values, cotangent, weights, decay_rates, conv, back, hin, gin, far)


def shards(query, key_in, values, cotangent, residues, decay_rates):
    devices = lax.axis_size("seq")
    rows, channels = query.shape
    modes, filters = decay_rates.shape
    groups = channels // filters
    share = groups * modes // devices
    scale = jnp.sqrt(-jnp.expm1(-2.0 * decay_rates))
    weights = residues * scale
    conv, back, hin, gin, states, slopes, sums = local_pass(
        query, key_in, values, cotangent, weights, decay_rates
    )
    if share == modes and modes % (devices // 2) == 0:
        far, zeroth, moment = exchange_pass(states, slopes, sums, decay_rates, float(rows))
    else:
        far, zeroth, moment = plain_exchange(states, slopes, sums, decay_rates, float(rows))
    query_grad, key_grad, value_grad = finish_pass(
        key_in, values, cotangent, weights, decay_rates, conv, back, hin, gin, far
    )
    norm_factor = 1.0 / math.sqrt(devices * rows)
    slope = jnp.exp(-2.0 * decay_rates) / scale
    residue_grad = scale * zeroth * norm_factor
    rate_grad = decay_rates * residues * (slope * zeroth - scale * moment) * norm_factor
    return (query_grad, key_grad, value_grad, residue_grad, rate_grad)


def solution(mesh):
    in_specs = (P("seq", "ch"), P("seq", "ch"), P("seq", "ch"), P("seq", "ch"), P(), P())
    out_specs = (P("seq", "ch"), P("seq", "ch"), P("seq", "ch"), P(), P())
    return jax.shard_map(shards, mesh=mesh, in_specs=in_specs, out_specs=out_specs, check_vma=False)
```

```python
import functools
import math

import jax
import jax.numpy as jnp
from jax import lax
from jax.experimental import pallas as pl
from jax.experimental.pallas import tpu as pltpu
from jax.sharding import PartitionSpec as P

SUBS = 8
LANES = 128
TILE = 4


def wide(row):
    return jnp.broadcast_to(row, (SUBS, LANES))


def fill_impulse(imp_ref, wgt_ref, dec_ref, length):
    modes = dec_ref.shape[0]
    lag = lax.broadcasted_iota(jnp.int32, (SUBS, LANES), 0)
    for block in range(length // SUBS):
        lags = (lag + block * SUBS).astype(jnp.float32)
        total = jnp.zeros((SUBS, LANES), jnp.float32)
        for m in range(modes):
            rate = dec_ref[m : m + 1, :]
            weight = wgt_ref[m : m + 1, :]
            total = total + weight * jnp.exp(-rate * lags)
        for i in range(SUBS):
            imp_ref[block * SUBS + i] = wide(total[i : i + 1, :])


def split_tokens(nat_ref, out_ref, length):
    for j in range(length):
        out_ref[j] = nat_ref[pl.ds(j, SUBS, stride=length), :]


def join_tokens(nat_ref, pieces, length):
    for j in range(length):
        nat_ref[pl.ds(j, SUBS, stride=length), :] = pieces[j]


def near_lags(u_ref, s_ref, imp_ref, conv, back, corr, length):
    tiles = length // TILE
    for j in range(length):
        conv[j] = jnp.zeros((SUBS, LANES), jnp.float32)
        back[j] = jnp.zeros((SUBS, LANES), jnp.float32)
    for delta in range(tiles):
        lags = [d for d in range(TILE * delta - TILE + 1, TILE * delta + TILE) if d >= 0]
        imp = {d: imp_ref[d] for d in lags}
        sums = {d: corr[d] for d in lags}
        for first in range(tiles - delta):
            sources = range(TILE * first, TILE * first + TILE)
            targets = range(TILE * (first + delta), TILE * (first + delta) + TILE)
            us = {s: u_ref[s] for s in sources}
            ss = {t: s_ref[t] for t in targets}
            cs = {t: conv[t] for t in targets}
            bs = {s: back[s] for s in sources}
            for t in targets:
                for s in sources:
                    if t >= s:
                        cs[t] = cs[t] + imp[t - s] * us[s]
                        bs[s] = bs[s] + imp[t - s] * ss[t]
                        sums[t - s] = sums[t - s] + us[s] * ss[t]
            for t in targets:
                conv[t] = cs[t]
            for s in sources:
                back[s] = bs[s]
        for d in lags:
            corr[d] = sums[d]


def block_states(u_ref, s_ref, dec_ref, modes, length):
    zero = jnp.zeros((SUBS, LANES), jnp.float32)
    decay = [wide(jnp.exp(-dec_ref[m : m + 1, :])) for m in modes]
    hs = [zero for _ in modes]
    h1s = [zero for _ in modes]
    gs = [zero for _ in modes]
    g1s = [zero for _ in modes]
    for j in range(length):
        u = u_ref[j]
        s = s_ref[length - 1 - j]
        for n in range(len(decay)):
            moved = decay[n] * hs[n]
            h1s[n] = decay[n] * h1s[n] + moved
            hs[n] = moved + u
            moved = decay[n] * gs[n]
            g1s[n] = decay[n] * g1s[n] + moved
            gs[n] = moved + s
    out = []
    for n in range(len(decay)):
        moved = decay[n] * hs[n]
        out.append((moved, decay[n] * h1s[n] + moved, gs[n], g1s[n]))
    return out


def local_kernel(
    length, k_ref, v_ref, g_ref, q_ref, wgt_ref, dec_ref,
    conv_ref, back_ref, hin_ref, gin_ref, state_ref, slope_ref, sums_ref,
    nat_ref, u_ref, s_ref, imp_ref, corr_ref, first_ref, second_ref,
):
    group = pl.program_id(0)
    modes = dec_ref.shape[0]

    @pl.when(group == 0)
    def _():
        fill_impulse(imp_ref, wgt_ref, dec_ref, length)
        corr_ref[...] = jnp.zeros_like(corr_ref)
        first_ref[...] = jnp.zeros_like(first_ref)
        second_ref[...] = jnp.zeros_like(second_ref)

    nat_ref[...] = k_ref[...].astype(jnp.float32) * v_ref[...].astype(jnp.float32)
    split_tokens(nat_ref, u_ref, length)
    nat_ref[...] = g_ref[...].astype(jnp.float32) * q_ref[...].astype(jnp.float32)
    split_tokens(nat_ref, s_ref, length)

    sub = lax.broadcasted_iota(jnp.int32, (SUBS, LANES), 0)
    half = modes // 2
    for start in range(0, modes, half):
        ids = range(start, start + half)
        for m, (h, h1, g, g1) in zip(ids, block_states(u_ref, s_ref, dec_ref, ids, length)):
            rate = wide(dec_ref[m : m + 1, :])
            ih, ih1, ig, ig1 = h, h1, g, g1
            step = 1
            while step < SUBS:
                span = float(step * length)
                power = jnp.exp(-span * rate)
                up = jnp.where(sub >= step, power, 0.0)
                down = jnp.where(sub < SUBS - step, power, 0.0)
                rh = pltpu.roll(ih, step, 0)
                rh1 = pltpu.roll(ih1, step, 0)
                ih1 = ih1 + up * (rh1 + span * rh)
                ih = ih + up * rh
                rg = pltpu.roll(ig, SUBS - step, 0)
                rg1 = pltpu.roll(ig1, SUBS - step, 0)
                ig1 = ig1 + down * (rg1 + span * rg)
                ig = ig + down * rg
                step *= 2
            hin = jnp.where(sub >= 1, pltpu.roll(ih, 1, 0), 0.0)
            h1in = jnp.where(sub >= 1, pltpu.roll(ih1, 1, 0), 0.0)
            gin = jnp.where(sub < SUBS - 1, pltpu.roll(ig, SUBS - 1, 0), 0.0)
            hin_ref[0, m] = hin
            gin_ref[0, m] = gin
            state_ref[0, 0, m : m + 1, :] = ih[SUBS - 1 :, :]
            state_ref[0, 1, m : m + 1, :] = ig[:1, :]
            slope_ref[0, 0, m : m + 1, :] = ih1[SUBS - 1 :, :]
            slope_ref[0, 1, m : m + 1, :] = ig1[:1, :]
            first_ref[m] += g * hin
            second_ref[m] += g1 * hin + g * h1in

    near_lags(u_ref, s_ref, imp_ref, conv_ref.at[0], back_ref.at[0], corr_ref, length)

    @pl.when(group == pl.num_programs(0) - 1)
    def _():
        corr = [jnp.sum(corr_ref[j], axis=0, keepdims=True) for j in range(length)]
        packs = [jnp.concatenate(corr[b : b + SUBS], axis=0) for b in range(0, length, SUBS)]
        for m in range(modes):
            rate = dec_ref[m : m + 1, :]
            first = first_ref[m]
            second = second_ref[m]
            for b in range(len(packs)):
                lags = (sub + b * SUBS).astype(jnp.float32)
                term = packs[b] * jnp.exp(-rate * lags)
                first = first + term
                second = second + term * lags
            sums_ref[0, m : m + 1, :] = jnp.sum(first, axis=0, keepdims=True)
            sums_ref[1, m : m + 1, :] = jnp.sum(second, axis=0, keepdims=True)


def local_pass(query, key_in, values, cotangent, weights, decay_rates):
    rows, channels = query.shape
    modes, filters = decay_rates.shape
    groups = channels // filters
    length = rows // SUBS
    column = pl.BlockSpec((rows, filters), lambda g: (0, g))
    small = pl.BlockSpec((modes, filters), lambda g: (0, 0))
    f32 = jnp.float32
    piece = pl.BlockSpec((1, length, SUBS, filters), lambda g: (g, 0, 0, 0))
    inner = pl.BlockSpec((1, modes, SUBS, filters), lambda g: (g, 0, 0, 0))
    pair = pl.BlockSpec((1, 2, modes, filters), lambda g: (g, 0, 0, 0))
    return pl.pallas_call(
        functools.partial(local_kernel, length),
        grid=(groups,),
        in_specs=[column] * 4 + [small] * 2,
        out_specs=[piece, piece, inner, inner, pair, pair,
                   pl.BlockSpec((2, modes, filters), lambda g: (0, 0, 0))],
        out_shape=[
            jax.ShapeDtypeStruct((groups, length, SUBS, filters), f32),
            jax.ShapeDtypeStruct((groups, length, SUBS, filters), f32),
            jax.ShapeDtypeStruct((groups, modes, SUBS, filters), f32),
            jax.ShapeDtypeStruct((groups, modes, SUBS, filters), f32),
            jax.ShapeDtypeStruct((groups, 2, modes, filters), f32),
            jax.ShapeDtypeStruct((groups, 2, modes, filters), f32),
            jax.ShapeDtypeStruct((2, modes, filters), f32),
        ],
        scratch_shapes=[
            pltpu.VMEM((rows, filters), f32),
            pltpu.VMEM((length, SUBS, filters), f32),
            pltpu.VMEM((length, SUBS, filters), f32),
            pltpu.VMEM((length, SUBS, filters), f32),
            pltpu.VMEM((length, SUBS, filters), f32),
            pltpu.VMEM((modes, SUBS, filters), f32),
            pltpu.VMEM((modes, SUBS, filters), f32),
        ],
        compiler_params=pltpu.CompilerParams(vmem_limit_bytes=60 * 1024 * 1024),
        name="local_pass",
    )(key_in, values, cotangent, query, weights, decay_rates)


def owner_kernel(span, x_ref, dec_ref, y_ref, first_ref, second_ref):
    devices = x_ref.shape[0]
    power = jnp.exp(-span * dec_ref[...])
    state = jnp.zeros_like(dec_ref[...])
    slope = state
    first = state
    second = state
    for d in range(devices):
        y_ref[d, 0] = state
        first = first + x_ref[d, 1] * state
        second = second + x_ref[d, 1] * slope
        slope = power * (slope + span * state)
        state = power * state + x_ref[d, 0]
    state = jnp.zeros_like(dec_ref[...])
    for d in reversed(range(devices)):
        y_ref[d, 1] = state
        state = power * state + x_ref[d, 1]
    first_ref[...] = first
    second_ref[...] = second


def owner_pass(received, rates, span):
    f32 = jnp.float32
    return pl.pallas_call(
        functools.partial(owner_kernel, span),
        out_shape=[
            jax.ShapeDtypeStruct(received.shape, f32),
            jax.ShapeDtypeStruct(rates.shape, f32),
            jax.ShapeDtypeStruct(rates.shape, f32),
        ],
        name="owner_pass",
    )(received, rates)


def exchange_kernel(
    span, x_ref, slope_ref, sums_ref, dec_ref, far_ref, total_ref,
    got, ans, back, part, red, mine, gath,
    send1, recv1, send2, recv2, send3, recv3, send4, recv4,
):
    devices = x_ref.shape[0]
    cores = gath.shape[0] // devices
    everyone = devices * cores
    me = lax.axis_index("seq")
    ch = lax.axis_index("ch")
    my = ch * devices + me
    mesh_ids = pl.DeviceIdType.MESH

    def seq_copy(source, target, sends, recvs, peer, slot):
        return pltpu.make_async_remote_copy(
            src_ref=source.at[peer], dst_ref=target.at[slot], send_sem=sends.at[peer],
            recv_sem=recvs.at[slot], device_id=(peer, ch), device_id_type=mesh_ids,
        )

    def swap_start(source, target, sends, recvs):
        def body(step, carry):
            peer = lax.rem(me + step, devices)
            seq_copy(source, target, sends, recvs, peer, me).start()
            return carry

        lax.fori_loop(1, devices, body, 0)

    def swap_wait(source, target, sends, recvs):
        def body(step, carry):
            peer = lax.rem(me + step, devices)
            seq_copy(source, target, sends, recvs, peer, peer).wait()
            return carry

        lax.fori_loop(1, devices, body, 0)

    barrier = pltpu.get_barrier_semaphore()

    def greet(step, carry):
        other = lax.rem(my + step, everyone)
        pl.semaphore_signal(
            barrier, inc=1, device_id=(lax.rem(other, devices), other // devices),
            device_id_type=mesh_ids,
        )
        return carry

    lax.fori_loop(1, everyone, greet, 0)
    pl.semaphore_wait(barrier, everyone - 1)

    swap_start(x_ref, got, send1, recv1)
    got[me] = x_ref[me]
    power = jnp.exp(-span * dec_ref[...])
    swap_wait(x_ref, got, send1, recv1)
    zero = jnp.zeros_like(power)
    state, slope, first, second = zero, zero, zero, zero
    for d in range(devices):
        ans[d, 0] = state
        first = first + got[d, 1] * state
        second = second + got[d, 1] * slope
        slope = power * (slope + span * state)
        state = power * state + got[d, 0]
    state = zero
    for d in reversed(range(devices)):
        ans[d, 1] = state
        state = power * state + got[d, 1]

    swap_start(ans, back, send2, recv2)
    back[me] = ans[me]
    swap_wait(ans, back, send2, recv2)
    first = first + sums_ref[0]
    second = second + sums_ref[1]
    for d in range(devices):
        second = second + slope_ref[d, 1] * back[d, 0] + slope_ref[d, 0] * back[d, 1]
        far_ref[d] = back[d]

    rows = part.shape[1]
    half = devices // 2
    for d in range(half):
        part[d] = first[d * rows : (d + 1) * rows, :]
        part[half + d] = second[d * rows : (d + 1) * rows, :]
    swap_start(part, red, send3, recv3)
    red[me] = part[me]
    swap_wait(part, red, send3, recv3)
    total = red[0]
    for d in range(1, devices):
        total = total + red[d]
    mine[...] = total
    gath[my] = total

    def all_copy(other, slot):
        return pltpu.make_async_remote_copy(
            src_ref=mine, dst_ref=gath.at[slot], send_sem=send4.at[other], recv_sem=recv4.at[slot],
            device_id=(lax.rem(other, devices), other // devices), device_id_type=mesh_ids,
        )

    def spread(step, carry):
        all_copy(lax.rem(my + step, everyone), my).start()
        return carry

    def collect(step, carry):
        other = lax.rem(my + step, everyone)
        all_copy(other, other).wait()
        return carry

    lax.fori_loop(1, everyone, spread, 0)
    lax.fori_loop(1, everyone, collect, 0)
    for d in range(devices):
        total = gath[d]
        for c in range(1, cores):
            total = total + gath[c * devices + d]
        total_ref[d] = total


def exchange_pass(states, slopes, sums, decay_rates, span):
    devices = lax.axis_size("seq")
    everyone = devices * lax.axis_size("ch")
    modes, filters = decay_rates.shape
    rows = 2 * modes // devices
    f32 = jnp.float32
    sem = pltpu.SemaphoreType.DMA
    vmem = pl.BlockSpec(memory_space=pltpu.VMEM)
    far, total = pl.pallas_call(
        functools.partial(exchange_kernel, span),
        in_specs=[vmem] * 4,
        out_specs=[vmem] * 2,
        out_shape=[
            jax.ShapeDtypeStruct(states.shape, f32),
            jax.ShapeDtypeStruct((devices, rows, filters), f32),
        ],
        scratch_shapes=[
            pltpu.VMEM(states.shape, f32),
            pltpu.VMEM(states.shape, f32),
            pltpu.VMEM(states.shape, f32),
            pltpu.VMEM((devices, rows, filters), f32),
            pltpu.VMEM((devices, rows, filters), f32),
            pltpu.VMEM((rows, filters), f32),
            pltpu.VMEM((everyone, rows, filters), f32),
        ]
        + [sem((devices,))] * 6
        + [sem((everyone,))] * 2,
        compiler_params=pltpu.CompilerParams(
            collective_id=0, has_side_effects=True, vmem_limit_bytes=60 * 1024 * 1024
        ),
        name="exchange_pass",
    )(states, slopes, sums, decay_rates)
    total = total.reshape(2, modes, filters)
    return far, total[0], total[1]


def plain_exchange(states, slopes, sums, decay_rates, span):
    devices = lax.axis_size("seq")
    me = lax.axis_index("seq")
    groups = states.shape[0]
    modes, filters = decay_rates.shape
    share = groups * modes // devices
    sent = states.transpose(0, 2, 1, 3).reshape(devices, share, 2, filters).transpose(0, 2, 1, 3)
    received = lax.all_to_all(sent, "seq", split_axis=0, concat_axis=0, tiled=True)
    row_rates = jnp.tile(decay_rates, (groups, 1)).reshape(devices, share, filters)
    own_rates = lax.dynamic_index_in_dim(row_rates, me, 0, keepdims=False)
    answer, first, second = owner_pass(received, own_rates, span)
    far = lax.all_to_all(answer, "seq", split_axis=0, concat_axis=0, tiled=True)
    far = far.transpose(0, 2, 1, 3).reshape(groups, modes, 2, filters).transpose(0, 2, 1, 3)
    crossing = jnp.sum(slopes[:, 1] * far[:, 0] + slopes[:, 0] * far[:, 1], axis=0)
    owned = jnp.zeros((2, groups * modes, filters), jnp.float32)
    owned = lax.dynamic_update_slice(owned, jnp.stack([first, second]), (0, me * share, 0))
    owned = owned.reshape(2, groups, modes, filters).sum(1)
    zeroth = sums[0] + owned[0]
    moment = sums[1] + owned[1] + crossing
    zeroth, moment = lax.psum((zeroth, moment), ("seq", "ch"))
    return far, zeroth, moment


def finish_kernel(
    length, k_ref, v_ref, g_ref, wgt_ref, dec_ref, conv_ref, back_ref, hin_ref, gin_ref, far_ref,
    dq_ref, dk_ref, dv_ref, nat_ref,
):
    modes = dec_ref.shape[0]
    sub = lax.broadcasted_iota(jnp.int32, (SUBS, LANES), 0).astype(jnp.float32)
    def total(parts):
        while len(parts) > 1:
            parts = [sum(parts[i : i + 2]) for i in range(0, len(parts), 2)]
        return parts[0]

    for i in range(conv_ref.shape[0]):
        cols = slice(i * LANES, (i + 1) * LANES)
        decay = []
        ahead = []
        behind = []
        for m in range(modes):
            rate = dec_ref[m : m + 1, :]
            weight = wgt_ref[m : m + 1, :]
            decay.append(wide(jnp.exp(-rate)))
            before = jnp.exp(-rate * (sub * float(length)))
            after = jnp.exp(-rate * ((SUBS - 1.0 - sub) * float(length)))
            ahead.append(weight * (hin_ref[i, m] + before * far_ref[i, 0, m : m + 1, :]))
            behind.append(weight * (gin_ref[i, m] + after * far_ref[i, 1, m : m + 1, :]))

        for j in range(length):
            nat_ref[pl.ds(j, SUBS, stride=length), :] = conv_ref[i, j] + total(ahead)
            ahead = [x * a for x, a in zip(ahead, decay)]
        dq_ref[:, cols] = (g_ref[:, cols].astype(jnp.float32) * nat_ref[...]).astype(jnp.bfloat16)
        for j in reversed(range(length)):
            behind = [x * a for x, a in zip(behind, decay)]
            nat_ref[pl.ds(j, SUBS, stride=length), :] = back_ref[i, j] + total(behind)
        dk_ref[:, cols] = (v_ref[:, cols].astype(jnp.float32) * nat_ref[...]).astype(jnp.bfloat16)
        dv_ref[:, cols] = (k_ref[:, cols].astype(jnp.float32) * nat_ref[...]).astype(jnp.bfloat16)


def finish_pass(key_in, values, cotangent, weights, decay_rates, conv, back, hin, gin, far):
    rows, channels = key_in.shape
    modes, filters = decay_rates.shape
    groups = channels // filters
    length = rows // SUBS
    per = 2 if groups % 2 == 0 else 1
    column = pl.BlockSpec((rows, per * filters), lambda g: (0, g))
    small = pl.BlockSpec((modes, filters), lambda g: (0, 0))
    piece = pl.BlockSpec((per, length, SUBS, filters), lambda g: (g, 0, 0, 0))
    inner = pl.BlockSpec((per, modes, SUBS, filters), lambda g: (g, 0, 0, 0))
    pair = pl.BlockSpec((per, 2, modes, filters), lambda g: (g, 0, 0, 0))
    return pl.pallas_call(
        functools.partial(finish_kernel, length),
        grid=(groups // per,),
        in_specs=[column] * 3 + [small] * 2 + [piece, piece, inner, inner, pair],
        out_specs=[column] * 3,
        out_shape=[jax.ShapeDtypeStruct((rows, channels), jnp.bfloat16)] * 3,
        scratch_shapes=[pltpu.VMEM((rows, filters), jnp.float32)],
        compiler_params=pltpu.CompilerParams(vmem_limit_bytes=60 * 1024 * 1024),
        name="finish_pass",
    )(key_in, values, cotangent, weights, decay_rates, conv, back, hin, gin, far)


def shards(query, key_in, values, cotangent, residues, decay_rates):
    devices = lax.axis_size("seq")
    rows, channels = query.shape
    modes, filters = decay_rates.shape
    groups = channels // filters
    share = groups * modes // devices
    scale = jnp.sqrt(-jnp.expm1(-2.0 * decay_rates))
    weights = residues * scale
    conv, back, hin, gin, states, slopes, sums = local_pass(
        query, key_in, values, cotangent, weights, decay_rates
    )
    if share == modes and modes % (devices // 2) == 0:
        far, zeroth, moment = exchange_pass(states, slopes, sums, decay_rates, float(rows))
    else:
        far, zeroth, moment = plain_exchange(states, slopes, sums, decay_rates, float(rows))
    query_grad, key_grad, value_grad = finish_pass(
        key_in, values, cotangent, weights, decay_rates, conv, back, hin, gin, far
    )
    norm_factor = 1.0 / math.sqrt(devices * rows)
    slope = jnp.exp(-2.0 * decay_rates) / scale
    residue_grad = scale * zeroth * norm_factor
    rate_grad = decay_rates * residues * (slope * zeroth - scale * moment) * norm_factor
    return (query_grad, key_grad, value_grad, residue_grad, rate_grad)


def solution(mesh):
    in_specs = (P("seq", "ch"), P("seq", "ch"), P("seq", "ch"), P("seq", "ch"), P(), P())
    out_specs = (P("seq", "ch"), P("seq", "ch"), P("seq", "ch"), P(), P())
    return jax.shard_map(shards, mesh=mesh, in_specs=in_specs, out_specs=out_specs, check_vma=False)
```
